256 devices in a mesh: rows: 4 (over y), seq: 64 (over z, x, core).
Axes of the slice: x: 4, y: 4, z: 8, core: 2. Of those that a mesh axis runs over, the one named last changes fastest.
Arguments:
- rollout_query: bfloat16 [32768, 24576], P(('rows', 'seq')), may hold values from -210 to 210
- rollout_latent: bfloat16 [32768, 576], P(('rows', 'seq')), may hold values from -40 to 40
- trainer_row: int32 [4, 8192], P(None, 'seq'), may hold values from 0 to 3, as said below
- segment_ids: int32 [4, 8192], P('rows'), may hold values from 0 to 63, never falling along the last dimension, each value on 1 to 256 neighbouring positions
- kv_gain: float32 [512], replicated, may hold values from 0.1 to 1.9
- key_up: bfloat16 [512, 16384], P(None, 'seq'), may hold values from -0.25 to 0.25
- value_up: bfloat16 [512, 16384], P(None, 'seq'), may hold values from -0.25 to 0.25
Outputs:
- attended: bfloat16 [32768, 16384], P(('rows', 'seq'))
The draws below stay inside these ranges and needn't reach their ends.
Inputs may be any that keep to these rules, and one draw needn't show every extreme that they name: `trainer_row`: for each seq index, each trainer row receives exactly 128 tokens from the 4 rollout devices of that seq index; at most 48 tokens go from one rollout device to one trainer row, and this bound is reached for every seq index. `segment_ids`: each response occupies at most 256 consecutive positions of a packed row.
All inputs are finite; a program needn't handle non-finite values.
Results may differ from the reference program's by a relative error of at most 0.0068.
Values may be sent and summed in bfloat16 or wider, within the bound.
A program may use at most 192 MiB of HBM per device.

```python
import math
import jax
import jax.numpy as jnp
import numpy as np
from jax import lax

HEADS = 128
QK_NOPE = 128
QK_ROPE = 64
V_HEAD = 128
LATENT = 512
TOK_DEV = 128
SEG_MOST = 256
ROW_LEN = 8192
QBLOCK = 512
TOKENS = 32768
N_ROWS = 4
N_SEQ = 64


def draw_rollout_latent(key, part):
    key = jax.random.fold_in(key, 7)
    first, second, third, fourth = jax.random.split(key, 4)
    row_scale = jnp.exp(jax.random.uniform(third, (TOKENS, 1), jnp.float32, -1.15, 1.15))
    col_scale = jnp.exp(jax.random.uniform(fourth, (1, LATENT), jnp.float32, -1.15, 1.15))
    latent_part = jnp.clip(jax.random.normal(first, (TOKENS, LATENT), jnp.float32), -4.0, 4.0)
    rotary_part = jnp.clip(jax.random.normal(second, (TOKENS, QK_ROPE), jnp.float32), -5.0, 5.0)
    latent_part = latent_part * row_scale * col_scale
    return jnp.concatenate([latent_part, rotary_part], 1).astype(jnp.bfloat16)


def draw_rollout_query(key, part):
    key = jax.random.fold_in(key, 9)
    first = jax.random.fold_in(key, 0)
    shape = (TOKENS, HEADS, QK_NOPE + QK_ROPE)
    base = jnp.clip(jax.random.normal(first, shape, jnp.float32), -5.0, 5.0)
    return base.reshape(TOKENS, HEADS * (QK_NOPE + QK_ROPE)).astype(jnp.bfloat16)


def draw_trainer_row(key, part):
    key = jax.random.fold_in(key, 5)
    first, second, third = jax.random.split(key, 3)
    num_rows = N_ROWS
    base_shift = jax.random.randint(first, (N_SEQ, 1, 1), 0, num_rows)
    step_shift = jax.random.randint(second, (N_SEQ, 1, 1), 1, num_rows)
    other_shift = (base_shift + step_shift) % num_rows
    source_ids = jnp.arange(num_rows, dtype=jnp.int32)[None, :, None]
    target_ids = jnp.arange(num_rows, dtype=jnp.int32)[None, None, :]
    plus_part = (target_ids == (source_ids + base_shift) % num_rows).astype(jnp.int32)
    minus_part = (target_ids == (source_ids + other_shift) % num_rows).astype(jnp.int32)
    counts = TOK_DEV // num_rows + TOK_DEV // 8 * (plus_part - minus_part)
    bounds = jnp.cumsum(counts, axis=-1)
    slots = jnp.arange(TOK_DEV, dtype=jnp.int32)
    targets = jnp.sum((slots[None, None, :, None] >= bounds[:, :, None, :]).astype(jnp.int32), axis=-1)
    perm_keys = jax.random.split(third, N_SEQ * num_rows)
    perms = jax.vmap(lambda single_key: jax.random.permutation(single_key, TOK_DEV))(perm_keys)
    perms = perms.reshape(N_SEQ, num_rows, TOK_DEV).astype(jnp.int32)
    targets = jnp.take_along_axis(targets, perms, axis=-1)
    return targets.transpose(1, 0, 2).reshape(num_rows, N_SEQ * TOK_DEV).astype(jnp.int32)


def block_levels(key, dims, cuts, smallest, largest):
    gain = 1.0
    for position, blocks in cuts:
        draws = jax.random.uniform(jax.random.fold_in(jax.random.fold_in(key, 6), position), (blocks,), jnp.float32, smallest / len(cuts), largest / len(cuts))
        gain = gain * jnp.repeat(jnp.exp(draws), dims[position] // blocks).reshape((-1,) + (1,) * (len(dims) - 1 - position))
    return gain


def length_profile(amount, total, limit, lean):
    loads = [(1 << 20) // math.isqrt(standing ** lean) + 1 for standing in range(2, amount + 1)]
    rest, given = total - limit - (amount - 1), [1] * (amount - 1)
    while rest > 0:
        movable = [i for i in range(amount - 1) if given[i] < limit]
        mass, budget = sum([loads[i] for i in movable]), rest
        for i in movable:
            addition = min(limit - given[i], max(1, budget * loads[i] // mass), rest)
            given[i] = given[i] + addition
            rest = rest - addition
    return np.array([limit] + given)


def uneven(own_key, amount, total, reach, lean):
    if amount == 2:
        one = jax.random.randint(own_key, (), max(1, total - reach), min(reach, total - 1) + 1)
        return jnp.stack([one, total - one])
    sizes = jnp.asarray(length_profile(amount, total, reach, lean), jnp.int32)
    twos = (amount - 1) // 2
    source_of, taker = sizes[1:1 + 2 * twos:2], sizes[2:2 + 2 * twos:2]
    margin = jnp.minimum(source_of - 1, reach - taker)
    passed = jax.random.randint(jax.random.fold_in(own_key, 1), (twos,), 0, 1 << 20) % (margin + 1)
    sizes = sizes.at[1:1 + 2 * twos:2].set(source_of - passed).at[2:2 + 2 * twos:2].set(taker + passed)
    return sizes[jax.random.permutation(jax.random.fold_in(own_key, 2), amount)]


def centred(key, extent, spread, most, pieces=(), held_as=jnp.bfloat16):
    loudness = block_levels(key, extent, pieces, -0.22, 0.18) if pieces else 1.0
    entries = jax.random.normal(key, extent, jnp.float32) * spread * loudness
    return jnp.minimum(jnp.maximum(entries, -most), most).astype(held_as)


def setup_inputs(seed: int = 0) -> dict:
    streams_of = jax.random.split(jax.random.key(seed), 8)
    return {
        "rollout_query": draw_rollout_query(jax.random.fold_in(streams_of[7], 71), 0),
        "rollout_latent": draw_rollout_latent(jax.random.fold_in(streams_of[7], 71), 0),
        "trainer_row": draw_trainer_row(jax.random.fold_in(streams_of[7], 71), 0),
        "segment_ids": jax.vmap(lambda own: jnp.searchsorted(jnp.cumsum(uneven(own, N_SEQ, ROW_LEN, SEG_MOST, 2)), jnp.arange(ROW_LEN), side="right"))(jax.random.split(streams_of[3], N_ROWS)).reshape((N_ROWS, ROW_LEN)).astype(jnp.int32),
        "kv_gain": jnp.clip(1.0 + 0.18 * jax.random.normal(streams_of[4], (LATENT,), jnp.float32), 0.1, 1.9),
        "key_up": centred(streams_of[5], (LATENT, HEADS * QK_NOPE), LATENT ** -0.5, 0.25, ((1, 64),)),
        "value_up": centred(streams_of[6], (LATENT, HEADS * V_HEAD), LATENT ** -0.5, 0.25, ((1, 64),)),
    }


def attend_rows(queries, keys, values, segment_row):
    span = SEG_MOST
    total = queries.shape[0]
    heads_here = queries.shape[1]
    scale = 1.0 / math.sqrt(QK_NOPE + QK_ROPE)
    padded_keys = jnp.concatenate([jnp.zeros((span, heads_here, keys.shape[2]), keys.dtype), keys], 0)
    padded_values = jnp.concatenate([jnp.zeros((span, heads_here, values.shape[2]), values.dtype), values], 0)
    padded_segments = jnp.concatenate([jnp.full((span,), -1, jnp.int32), segment_row.astype(jnp.int32)], 0)

    def one_block(block_index):
        begin_row = (block_index * QBLOCK).astype(jnp.int32)
        query_block = lax.dynamic_slice_in_dim(queries, begin_row, QBLOCK, 0)
        key_block = lax.dynamic_slice_in_dim(padded_keys, begin_row, QBLOCK + span, 0)
        value_block = lax.dynamic_slice_in_dim(padded_values, begin_row, QBLOCK + span, 0)
        query_segments = lax.dynamic_slice_in_dim(padded_segments, begin_row + span, QBLOCK, 0)
        key_segments = lax.dynamic_slice_in_dim(padded_segments, begin_row, QBLOCK + span, 0)
        scores = jnp.einsum('qhd,khd->hqk', query_block.astype(jnp.float32), key_block.astype(jnp.float32)) * scale
        query_pos = begin_row + jnp.arange(QBLOCK, dtype=jnp.int32)
        key_pos = begin_row - span + jnp.arange(QBLOCK + span, dtype=jnp.int32)
        allowed = (query_segments[:, None] == key_segments[None, :]) & (key_pos[None, :] <= query_pos[:, None])
        scores = jnp.where(allowed[None], scores, -1e+30)
        top_score = lax.optimization_barrier(jnp.max(scores, axis=-1, keepdims=True))
        weights = jnp.exp(scores - top_score)
        weights = (weights / lax.optimization_barrier(jnp.sum(weights, axis=-1, keepdims=True))).astype(jnp.bfloat16)
        mixed = jnp.einsum('hqk,khd->qhd', weights.astype(jnp.float32), value_block.astype(jnp.float32))
        return mixed.astype(jnp.bfloat16)
    blocks = lax.map(one_block, jnp.arange(total // QBLOCK, dtype=jnp.int32))
    return blocks.reshape(total, heads_here, values.shape[2])

def normalize_latent(latent_rows, kv_gain):
    latent_part = latent_rows[:, :LATENT].astype(jnp.float32)
    inverse_rms = lax.rsqrt(lax.optimization_barrier(jnp.mean(latent_part * latent_part, axis=-1, keepdims=True)) + 1e-06)
    normed = (latent_part * inverse_rms * kv_gain).astype(jnp.bfloat16)
    return jnp.concatenate([normed, latent_rows[:, LATENT:]], 1)

def reference(rollout_query, rollout_latent, trainer_row, segment_ids, kv_gain, key_up, value_up):
    per_row = TOK_DEV
    targets = trainer_row.reshape(N_ROWS, N_SEQ, per_row).transpose(1, 0, 2).reshape(N_SEQ, N_ROWS * per_row)
    order = jnp.argsort(targets, axis=1, stable=True).astype(jnp.int32)
    seq_index = jnp.arange(N_SEQ, dtype=jnp.int32)[:, None]
    source = (order // per_row * N_SEQ + seq_index) * per_row + order % per_row
    source = source.reshape(N_SEQ, N_ROWS, per_row).transpose(1, 0, 2).reshape(TOKENS).astype(jnp.int32)
    packed_query = rollout_query[source]
    packed_latent = rollout_latent[source]
    head_width = QK_NOPE + QK_ROPE
    results = []
    for row_index in range(N_ROWS):
        query_row = packed_query[row_index * ROW_LEN:(row_index + 1) * ROW_LEN].reshape(ROW_LEN, HEADS, head_width)
        latent_norm = normalize_latent(packed_latent[row_index * ROW_LEN:(row_index + 1) * ROW_LEN], kv_gain)
        latent_part = latent_norm[:, :LATENT]
        rotary_key = latent_norm[:, LATENT:]
        segment_row = segment_ids[row_index]

        def per_head(head_index):
            key_cols = lax.dynamic_slice_in_dim(key_up, head_index * QK_NOPE, QK_NOPE, 1)
            value_cols = lax.dynamic_slice_in_dim(value_up, head_index * V_HEAD, V_HEAD, 1)
            key_nope = jnp.dot(latent_part, key_cols, preferred_element_type=jnp.float32).astype(jnp.bfloat16)
            values = jnp.dot(latent_part, value_cols, preferred_element_type=jnp.float32).astype(jnp.bfloat16)
            keys = jnp.concatenate([key_nope, rotary_key], 1)[:, None, :]
            head_query = lax.dynamic_slice_in_dim(query_row, head_index, 1, 1)
            return attend_rows(head_query, keys, values[:, None, :], segment_row)[:, 0, :]
        head_outputs = lax.map(per_head, jnp.arange(HEADS, dtype=jnp.int32))
        results.append(head_outputs.transpose(1, 0, 2).reshape(ROW_LEN, HEADS * V_HEAD))
    return jnp.concatenate(results, 0)
```

```python
import math

import jax
import jax.numpy as jnp
from jax import lax
from jax.experimental import pallas as pl
from jax.experimental.pallas import tpu as pltpu
from jax.sharding import PartitionSpec as P

HEADS = 128
QK_NOPE = 128
QK_ROPE = 64
V_HEAD = 128
LATENT = 512
TOK = 128
ROWS = 4
X_CHIPS = 4
Z_CHIPS = 8
STEPS = 8
LOOK = 8
PAIR_Q = 2 * (QK_NOPE + QK_ROPE)
PAIR_V = 2 * V_HEAD
WIDE = LATENT + 2 * QK_ROPE
SPAN = 3 * TOK
WINDOW = 4 * TOK
SCALE = math.log2(math.e) / math.sqrt(QK_NOPE + QK_ROPE)
MESH = pl.DeviceIdType.MESH
F32 = jnp.float32
BF16 = jnp.bfloat16


def kernel(
    q_ref, lat_ref, tgt_ref, seg_ref, gain_ref, ku_ref, vu_ref, out_ref,
    gath, tgts, segs, lat4, perm, bias, rope_hi, w_own, w_buf, q_buf, o_buf, ka_buf, kb_buf, v_buf,
    gath_s, gath_r, seg_s, seg_r, tgt_s, tgt_r, halo_s, halo_r,
    w_s, w_r, q_s, q_r, o_s, o_r,
):
    r = lax.axis_index("rows")
    s = lax.axis_index("seq")
    c = lax.rem(s, 2)
    chip = s // 2
    x = lax.rem(chip, X_CHIPS)
    z = chip // X_CHIPS

    def at(row, zz, xx, core):
        return (row, (zz * X_CHIPS + xx) * 2 + core)

    sib = (r, chip * 2 + (1 - c))
    next_chip = (r, lax.rem(chip + 1, X_CHIPS * Z_CHIPS) * 2 + c)
    prev_chip = (r, lax.rem(chip + X_CHIPS * Z_CHIPS - 1, X_CHIPS * Z_CHIPS) * 2 + c)
    z_up = at(r, lax.rem(z + 1, Z_CHIPS), x, c)
    z_down = at(r, lax.rem(z + Z_CHIPS - 1, Z_CHIPS), x, c)
    x_to = at(r, z, lax.rem(x + X_CHIPS - r, X_CHIPS), c)
    x_from = at(r, z, lax.rem(x + r, X_CHIPS), c)
    group = [
        (dr, dc, lax.rem(r + dr, ROWS), lax.rem(c + dc, 2))
        for dr in range(ROWS)
        for dc in range(2)
        if (dr, dc) != (0, 0)
    ]

    barrier = pltpu.get_barrier_semaphore()
    for _, _, row, core in group:
        pl.semaphore_signal(barrier, 1, device_id=at(row, z, x, core), device_id_type=MESH)
    for peer in (next_chip, prev_chip, z_up, z_down):
        pl.semaphore_signal(barrier, 1, device_id=peer, device_id_type=MESH)

    @pl.when(r != 0)
    def _():
        for peer in (x_to, x_from):
            pl.semaphore_signal(barrier, 1, device_id=peer, device_id_type=MESH)

    def source_seq(t, row, core):
        up = lax.rem(t, 2)
        off = up * ((t + 1) // 2) - (1 - up) * (t // 2)
        z_src = lax.rem(z + off + Z_CHIPS, Z_CHIPS)
        return z_src * (2 * X_CHIPS) + lax.rem(row + x, X_CHIPS) * 2 + core

    raw = lat_ref[:, :LATENT].astype(F32)
    inverse = lax.rsqrt(jnp.mean(raw * raw, axis=1, keepdims=True) + 1e-06)
    gath[r, :, :LATENT] = (raw * inverse * gain_ref[...]).astype(BF16)
    gath[r, :, LATENT:] = jnp.concatenate(
        [lat_ref[:, LATENT:], jnp.zeros((TOK, QK_ROPE), BF16)], axis=1
    )
    w_own[:, :128] = ku_ref[:, :128]
    w_own[:, 128:256] = pltpu.roll(ku_ref[:, 128:].astype(F32), 64, 1).astype(BF16)
    w_own[:, 256:] = vu_ref[...]
    tgts[c] = jnp.concatenate([tgt_ref[i : i + 1, :] for i in range(ROWS)], axis=1)
    before = pl.multiple_of(jnp.maximum(chip - 1, 0) * 2 * TOK, 2 * TOK)
    segs[r, :, : 2 * TOK] = seg_ref[:, pl.ds(before, 2 * TOK)]
    segs[r, :, 2 * TOK :] = seg_ref[:, pl.ds(pl.multiple_of(chip * 2 * TOK, 2 * TOK), 2 * TOK)]

    @pl.when(r != 0)
    def _():
        pl.semaphore_wait(barrier, 13)

    @pl.when(r == 0)
    def _():
        pl.semaphore_wait(barrier, 11)

    def remote(src, dst, send, recv, peer):
        return pltpu.make_async_remote_copy(
            src_ref=src, dst_ref=dst, send_sem=send, recv_sem=recv,
            device_id=peer, device_id_type=MESH,
        )

    def lat_copy(dr):
        peer = at(lax.rem(r + dr, ROWS), z, x, c)
        return remote(gath.at[r], gath.at[r], gath_s.at[dr - 1], gath_r.at[dr - 1], peer)

    def seg_copy(dr):
        peer = at(lax.rem(r + dr, ROWS), z, x, c)
        return remote(segs.at[r], segs.at[r], seg_s.at[dr - 1], seg_r.at[dr - 1], peer)

    tgt_copy = remote(tgts.at[c], tgts.at[c], tgt_s, tgt_r, sib)
    for dr in (1, 3, 2):
        lat_copy(dr).start()
    tgt_copy.start()
    for dr in (1, 3, 2):
        seg_copy(dr).start()

    w_first = remote(w_own, w_buf.at[0], w_s.at[0], w_r.at[0], x_to)

    @pl.when(r != 0)
    def _():
        w_first.start()

    @pl.when(r == 0)
    def _():
        pltpu.make_async_copy(w_own, w_buf.at[0], w_r.at[0]).start()

    def w_wait(t):
        pltpu.make_async_copy(w_buf.at[t], w_buf.at[t], w_r.at[t]).wait()

    def w_copy(src, dst, peer):
        return remote(w_buf.at[src], w_buf.at[dst], w_s.at[dst], w_r.at[dst], peer)

    def q_copy(t, i):
        dr, dc, row, core = group[i]
        cols = pl.ds(pl.multiple_of(source_seq(t, row, core) * PAIR_Q, 128), PAIR_Q)
        return remote(
            q_ref.at[:, cols], q_buf.at[t, c, r], q_s.at[t, i], q_r.at[t], at(row, z, x, core)
        )

    def q_start(t):
        for i in (0, 1, 5, 2, 6, 3, 4):
            q_copy(t, i).start()
        cols = pl.ds(pl.multiple_of(source_seq(t, r, c) * PAIR_Q, 128), PAIR_Q)
        pltpu.make_async_copy(q_ref.at[:, cols], q_buf.at[t, c, r], q_r.at[t]).start()

    def q_first(t, carry):
        q_start(t)
        return carry

    lax.fori_loop(0, LOOK, q_first, 0)

    def fill_perm(core):
        targets = tgts[core]
        row_ids = lax.broadcasted_iota(jnp.int32, (8, WINDOW), 0)
        hot = (targets == row_ids).astype(F32)
        earlier = (
            lax.broadcasted_iota(jnp.int32, (WINDOW, WINDOW), 0)
            < lax.broadcasted_iota(jnp.int32, (WINDOW, WINDOW), 1)
        ).astype(F32)
        counts = jnp.dot(
            hot.astype(BF16), earlier.astype(BF16), preferred_element_type=F32
        )
        rank = jnp.sum(hot * counts, axis=0, keepdims=True).astype(jnp.int32)
        slot = targets * TOK + rank
        perm[core] = (
            lax.broadcasted_iota(jnp.int32, (WINDOW, WINDOW), 0) == slot
        ).astype(F32).astype(BF16)

    fill_perm(c)
    for dr in (1, 3, 2):
        lat_copy(dr).wait_recv()
    lat4[2 + c] = jnp.dot(
        perm[c], gath[...].reshape(WINDOW, WIDE), preferred_element_type=F32
    ).astype(BF16)
    own_next = remote(lat4.at[2 + c], lat4.at[c], halo_s.at[0], halo_r.at[0], next_chip)
    own_sib = remote(lat4.at[2 + c], lat4.at[2 + c], halo_s.at[1], halo_r.at[1], sib)
    fwd_sib = remote(lat4.at[c], lat4.at[c], halo_s.at[2], halo_r.at[2], sib)
    own_next.start()
    own_sib.start()

    w_wait(0)
    w_copy(0, 1, z_down).start()
    w_copy(0, 2, z_up).start()

    tgt_copy.wait_recv()
    fill_perm(1 - c)
    for dr in (1, 3, 2):
        seg_copy(dr).wait_recv()

    eye = lax.broadcasted_iota(jnp.int32, (TOK, TOK), 0) == lax.broadcasted_iota(
        jnp.int32, (TOK, TOK), 1
    )
    for core in range(2):
        key_pos = lax.broadcasted_iota(jnp.int32, (TOK, SPAN), 1)
        query_pos = lax.broadcasted_iota(jnp.int32, (TOK, SPAN), 0) + 2 * TOK
        there = (key_pos + core * TOK + chip * 1024) >= 2 * TOK
        causal = (key_pos <= query_pos) & there
        for row in range(ROWS):
            seg = segs[row].astype(F32)
            seg_k = seg[:, core * TOK : core * TOK + SPAN]
            seg_q = jnp.sum(
                jnp.where(eye, seg[:, (2 + core) * TOK : (3 + core) * TOK], 0.0),
                axis=1,
                keepdims=True,
            )
            bias[core, row] = jnp.where((seg_q == seg_k) & causal, 0.0, -1e30)

    own_next.wait_recv()
    fwd_sib.start()
    own_sib.wait_recv()
    fwd_sib.wait_recv()
    for row in range(ROWS):
        tile = lat4[:, row * TOK : (row + 1) * TOK, LATENT:].reshape(WINDOW, 128)
        rope_hi[row] = pltpu.roll(tile.astype(F32), 64, 1)

    low = lax.broadcasted_iota(jnp.int32, (WINDOW, 128), 1) < 64

    def o_copy(t, row, core):
        cols = pl.ds(pl.multiple_of(source_seq(t, r, c) * PAIR_V, 128), PAIR_V)
        return remote(
            o_buf.at[t, core, row], out_ref.at[:, cols], o_s.at[t, core, row], o_r.at[t],
            at(row, z, x, core),
        )

    def step(t, carry):
        @pl.when(t > 0)
        def _():
            w_wait(t)

        @pl.when((t > 0) & (t < STEPS - 2) & (lax.rem(t, 2) == 1))
        def _():
            w_copy(t, t + 2, z_down).start()

        @pl.when((t > 0) & (t < STEPS - 2) & (lax.rem(t, 2) == 0))
        def _():
            w_copy(t, t + 2, z_up).start()

        @pl.when(t + LOOK < STEPS)
        def _():
            q_start(t + LOOK)

        pltpu.make_async_copy(q_buf.at[t], q_buf.at[t], q_r.at[t]).wait()

        def one_row(row, carry):
            rows = pl.ds(pl.multiple_of(row * TOK, TOK), TOK)
            lat = lat4[:, rows, :].reshape(WINDOW, WIDE)
            kv = jnp.dot(lat[:, :LATENT], w_buf[t], preferred_element_type=F32)
            ka_buf[:, :128] = kv[:, :128].astype(BF16)
            ka_buf[:, 128:] = lat[:, LATENT:]
            kb = kv[:, 128:256]
            kb_buf[:, :128] = jnp.where(low, 0.0, kb).astype(BF16)
            kb_buf[:, 128:] = jnp.where(low, kb, rope_hi[row]).astype(BF16)
            v_buf[...] = kv[:, 256:].astype(BF16)
            for core in range(2):
                q = jnp.dot(
                    perm[core, rows, :],
                    q_buf[t, core].reshape(WINDOW, PAIR_Q),
                    preferred_element_type=F32,
                ).astype(BF16)
                keys = slice(core * TOK, core * TOK + SPAN)
                for head, k_buf in ((0, ka_buf), (1, kb_buf)):
                    scores = lax.dot_general(
                        q[:, head * 128 : head * 128 + 256], k_buf[keys, :],
                        (((1,), (1,)), ((), ())), preferred_element_type=F32,
                    )
                    scores = scores * SCALE + bias[core, row]
                    top = jnp.max(scores, axis=1, keepdims=True)
                    weights = jnp.exp2(scores - top)
                    total = jnp.sum(weights, axis=1, keepdims=True)
                    probs = (weights * (1.0 / total)).astype(BF16)
                    mixed = jnp.dot(
                        probs, v_buf[keys, head * 128 : (head + 1) * 128],
                        preferred_element_type=F32,
                    )
                    o_buf[t, core, row, :, head * 128 : (head + 1) * 128] = mixed.astype(BF16)
                own = (row == r) & (c == core)

                @pl.when(jnp.logical_not(own))
                def _():
                    o_copy(t, row, core).start()

                @pl.when(own)
                def _():
                    cols = pl.ds(pl.multiple_of(source_seq(t, r, c) * PAIR_V, 128), PAIR_V)
                    pltpu.make_async_copy(
                        o_buf.at[t, core, row], out_ref.at[:, cols], o_r.at[t]
                    ).start()
            return carry

        lax.fori_loop(0, ROWS, one_row, 0)
        return carry

    lax.fori_loop(0, STEPS, step, 0)

    for dr in (1, 3, 2):
        lat_copy(dr).wait_send()
        seg_copy(dr).wait_send()
    tgt_copy.wait_send()
    own_next.wait_send()
    own_sib.wait_send()
    fwd_sib.wait_send()

    @pl.when(r != 0)
    def _():
        w_first.wait_send()

    def w_drain(t, carry):
        w_copy(0, t, z_down).wait_send()
        return carry

    lax.fori_loop(1, STEPS, w_drain, 0)

    def drain(t, carry):
        for i in range(7):
            q_copy(t, i).wait_send()
        for dr, dc, row, core in group:
            o_copy(t, row, core).wait_send()
        done = out_ref.at[:, pl.ds(pl.multiple_of(t * 8 * PAIR_V, 128), 8 * PAIR_V)]
        pltpu.make_async_copy(done, done, o_r.at[t]).wait()
        return carry

    lax.fori_loop(0, STEPS, drain, 0)


def local(rollout_query, rollout_latent, trainer_row, segment_ids, kv_gain, key_up, value_up):
    vmem = pl.BlockSpec(memory_space=pltpu.VMEM)
    hbm = pl.BlockSpec(memory_space=pl.ANY)
    dma = pltpu.SemaphoreType.DMA
    return pl.pallas_call(
        kernel,
        out_shape=jax.ShapeDtypeStruct((TOK, HEADS * V_HEAD), BF16),
        in_specs=[hbm] + [vmem] * 6,
        out_specs=hbm,
        scratch_shapes=[
            pltpu.VMEM((ROWS, TOK, WIDE), BF16),
            pltpu.VMEM((2, 1, WINDOW), jnp.int32),
            pltpu.VMEM((ROWS, 1, WINDOW), jnp.int32),
            pltpu.VMEM((4, WINDOW, WIDE), BF16),
            pltpu.VMEM((2, WINDOW, WINDOW), BF16),
            pltpu.VMEM((2, ROWS, TOK, SPAN), F32),
            pltpu.VMEM((ROWS, WINDOW, 128), F32),
            pltpu.VMEM((LATENT, 512), BF16),
            pltpu.VMEM((STEPS, LATENT, 512), BF16),
            pltpu.VMEM((STEPS, 2, ROWS, TOK, PAIR_Q), BF16),
            pltpu.VMEM((STEPS, 2, ROWS, TOK, PAIR_V), BF16),
            pltpu.VMEM((WINDOW, 256), BF16),
            pltpu.VMEM((WINDOW, 256), BF16),
            pltpu.VMEM((WINDOW, 256), BF16),
            dma((3,)), dma((3,)), dma((3,)), dma((3,)), dma, dma, dma((3,)), dma((3,)),
            dma((STEPS,)), dma((STEPS,)), dma((STEPS, 7)), dma((STEPS,)), dma((STEPS, 2, ROWS)),
            dma((STEPS,)),
        ],
        compiler_params=pltpu.CompilerParams(
            collective_id=0, has_side_effects=True, vmem_limit_bytes=56 << 20
        ),
        cost_estimate=pl.CostEstimate(
            flops=18_000_000_000, bytes_accessed=24_000_000, transcendentals=6_500_000
        ),
    )(
        rollout_query, rollout_latent, trainer_row, segment_ids, kv_gain.reshape(1, LATENT),
        key_up, value_up,
    )


def solution(mesh):
    placed = (
        P(("rows", "seq"), None),
        P(("rows", "seq"), None),
        P(None, "seq"),
        P("rows", None),
        P(),
        P(None, "seq"),
        P(None, "seq"),
    )
    return jax.shard_map(
        local, mesh=mesh, in_specs=placed, out_specs=P(("rows", "seq"), None), check_vma=False
    )
```

```python
import math

import jax
import jax.numpy as jnp
from jax import lax
from jax.experimental import pallas as pl
from jax.experimental.pallas import tpu as pltpu
from jax.sharding import PartitionSpec as P

HEADS = 128
QK_NOPE = 128
QK_ROPE = 64
V_HEAD = 128
LATENT = 512
TOK = 128
ROWS = 4
X_CHIPS = 4
Z_CHIPS = 8
STEPS = 8
LOOK = 8
PAIR_Q = 2 * (QK_NOPE + QK_ROPE)
PAIR_V = 2 * V_HEAD
WIDE = LATENT + 2 * QK_ROPE
SPAN = 3 * TOK
WINDOW = 4 * TOK
SCALE = math.log2(math.e) / math.sqrt(QK_NOPE + QK_ROPE)
MESH = pl.DeviceIdType.MESH
F32 = jnp.float32
BF16 = jnp.bfloat16
NT = (((1,), (1,)), ((), ()))


def dot(a, b):
    return jnp.dot(a, b, preferred_element_type=F32)


def dot_nt(a, b):
    return lax.dot_general(a, b, NT, preferred_element_type=F32)


def kernel(
    q_ref, lat_ref, tgt_ref, seg_ref, gain_ref, ku_ref, vu_ref, out_ref,
    gath, tgts, segs, lat4, perm, bias, rope_hi, w_own, w_buf, q_buf, o_buf, ka_buf, kb_buf, vt_buf, qp_buf,
    gath_s, gath_r, seg_s, seg_r, tgt_s, tgt_r, halo_s, halo_r,
    w_s, w_r, q_s, q_r, o_s, o_r,
):
    r = lax.axis_index("rows")
    s = lax.axis_index("seq")
    c = lax.rem(s, 2)
    chip = s // 2
    x = lax.rem(chip, X_CHIPS)
    z = chip // X_CHIPS

    def at(row, zz, xx, core):
        return (row, (zz * X_CHIPS + xx) * 2 + core)

    sib = (r, chip * 2 + (1 - c))
    next_chip = (r, lax.rem(chip + 1, X_CHIPS * Z_CHIPS) * 2 + c)
    prev_chip = (r, lax.rem(chip + X_CHIPS * Z_CHIPS - 1, X_CHIPS * Z_CHIPS) * 2 + c)
    z_up = at(r, lax.rem(z + 1, Z_CHIPS), x, c)
    z_down = at(r, lax.rem(z + Z_CHIPS - 1, Z_CHIPS), x, c)
    x_to = at(r, z, lax.rem(x + X_CHIPS - r, X_CHIPS), c)
    x_from = at(r, z, lax.rem(x + r, X_CHIPS), c)
    group = [
        (dr, dc, lax.rem(r + dr, ROWS), lax.rem(c + dc, 2))
        for dr in range(ROWS)
        for dc in range(2)
        if (dr, dc) != (0, 0)
    ]

    barrier = pltpu.get_barrier_semaphore()
    for _, _, row, core in group:
        pl.semaphore_signal(barrier, 1, device_id=at(row, z, x, core), device_id_type=MESH)
    for peer in (next_chip, prev_chip, z_up, z_down):
        pl.semaphore_signal(barrier, 1, device_id=peer, device_id_type=MESH)

    @pl.when(r != 0)
    def _():
        for peer in (x_to, x_from):
            pl.semaphore_signal(barrier, 1, device_id=peer, device_id_type=MESH)

    def source_seq(t, row, core):
        up = lax.rem(t, 2)
        off = up * ((t + 1) // 2) - (1 - up) * (t // 2)
        z_src = lax.rem(z + off + Z_CHIPS, Z_CHIPS)
        return z_src * (2 * X_CHIPS) + lax.rem(row + x, X_CHIPS) * 2 + core

    raw = lat_ref[:, :LATENT].astype(F32)
    inverse = lax.rsqrt(jnp.mean(raw * raw, axis=1, keepdims=True) + 1e-06)
    gath[r, :, :LATENT] = (raw * inverse * gain_ref[...]).astype(BF16)
    gath[r, :, LATENT:] = jnp.concatenate(
        [lat_ref[:, LATENT:], jnp.zeros((TOK, QK_ROPE), BF16)], axis=1
    )
    w_own[:, :128] = ku_ref[:, :128]
    w_own[:, 128:256] = pltpu.roll(ku_ref[:, 128:].astype(F32), 64, 1).astype(BF16)
    turned = vu_ref[...].astype(F32).T.astype(BF16)
    w_own[:256, 256:] = turned[:, :256]
    w_own[256:, 256:] = turned[:, 256:]
    tgts[c] = jnp.concatenate([tgt_ref[i : i + 1, :] for i in range(ROWS)], axis=1)
    before = pl.multiple_of(jnp.maximum(chip - 1, 0) * 2 * TOK, 2 * TOK)
    segs[r, :, : 2 * TOK] = seg_ref[:, pl.ds(before, 2 * TOK)]
    segs[r, :, 2 * TOK :] = seg_ref[:, pl.ds(pl.multiple_of(chip * 2 * TOK, 2 * TOK), 2 * TOK)]

    @pl.when(r != 0)
    def _():
        pl.semaphore_wait(barrier, 13)

    @pl.when(r == 0)
    def _():
        pl.semaphore_wait(barrier, 11)

    def remote(src, dst, send, recv, peer):
        return pltpu.make_async_remote_copy(
            src_ref=src, dst_ref=dst, send_sem=send, recv_sem=recv,
            device_id=peer, device_id_type=MESH,
        )

    def lat_copy(dr):
        peer = at(lax.rem(r + dr, ROWS), z, x, c)
        return remote(gath.at[r], gath.at[r], gath_s.at[dr - 1], gath_r.at[dr - 1], peer)

    def seg_copy(dr):
        peer = at(lax.rem(r + dr, ROWS), z, x, c)
        return remote(segs.at[r], segs.at[r], seg_s.at[dr - 1], seg_r.at[dr - 1], peer)

    tgt_copy = remote(tgts.at[c], tgts.at[c], tgt_s, tgt_r, sib)
    for dr in (1, 3, 2):
        lat_copy(dr).start()
    tgt_copy.start()
    for dr in (1, 3, 2):
        seg_copy(dr).start()

    w_first = remote(w_own, w_buf.at[0], w_s.at[0], w_r.at[0], x_to)

    @pl.when(r != 0)
    def _():
        w_first.start()

    @pl.when(r == 0)
    def _():
        pltpu.make_async_copy(w_own, w_buf.at[0], w_r.at[0]).start()

    def w_wait(t):
        pltpu.make_async_copy(w_buf.at[t], w_buf.at[t], w_r.at[t]).wait()

    def w_copy(src, dst, peer):
        return remote(w_buf.at[src], w_buf.at[dst], w_s.at[dst], w_r.at[dst], peer)

    def q_copy(t, i):
        dr, dc, row, core = group[i]
        cols = pl.ds(pl.multiple_of(source_seq(t, row, core) * PAIR_Q, 128), PAIR_Q)
        return remote(
            q_ref.at[:, cols], q_buf.at[t, c, r], q_s.at[t, i], q_r.at[t], at(row, z, x, core)
        )

    def q_start(t):
        for i in (0, 1, 5, 2, 6, 3, 4):
            q_copy(t, i).start()
        cols = pl.ds(pl.multiple_of(source_seq(t, r, c) * PAIR_Q, 128), PAIR_Q)
        pltpu.make_async_copy(q_ref.at[:, cols], q_buf.at[t, c, r], q_r.at[t]).start()

    def q_first(t, carry):
        q_start(t)
        return carry

    lax.fori_loop(0, LOOK, q_first, 0)

    def fill_perm(core):
        targets = tgts[core]
        row_ids = lax.broadcasted_iota(jnp.int32, (8, WINDOW), 0)
        hot = (targets == row_ids).astype(F32)
        earlier = (
            lax.broadcasted_iota(jnp.int32, (WINDOW, WINDOW), 0)
            < lax.broadcasted_iota(jnp.int32, (WINDOW, WINDOW), 1)
        ).astype(F32)
        counts = jnp.dot(
            hot.astype(BF16), earlier.astype(BF16), preferred_element_type=F32
        )
        rank = jnp.sum(hot * counts, axis=0, keepdims=True).astype(jnp.int32)
        slot = targets * TOK + rank
        perm[core] = (
            lax.broadcasted_iota(jnp.int32, (WINDOW, WINDOW), 0) == slot
        ).astype(F32).astype(BF16)

    fill_perm(c)
    for dr in (1, 3, 2):
        lat_copy(dr).wait_recv()
    lat4[2 + c] = jnp.dot(
        perm[c], gath[...].reshape(WINDOW, WIDE), preferred_element_type=F32
    ).astype(BF16)
    own_next = remote(lat4.at[2 + c], lat4.at[c], halo_s.at[0], halo_r.at[0], next_chip)
    own_sib = remote(lat4.at[2 + c], lat4.at[2 + c], halo_s.at[1], halo_r.at[1], sib)
    fwd_sib = remote(lat4.at[c], lat4.at[c], halo_s.at[2], halo_r.at[2], sib)
    own_next.start()
    own_sib.start()

    w_wait(0)
    w_copy(0, 1, z_down).start()
    w_copy(0, 2, z_up).start()

    tgt_copy.wait_recv()
    fill_perm(1 - c)
    for dr in (1, 3, 2):
        seg_copy(dr).wait_recv()

    first_key = jnp.where(chip > 0, 0, 2 * TOK)
    for row in range(ROWS):
        seg = segs[row].astype(F32)
        seg_k = jnp.broadcast_to(seg, (8, WINDOW)).T[:, :1]
        for core in range(2):
            key_pos = lax.broadcasted_iota(jnp.int32, (SPAN, TOK), 0) + core * TOK
            query_pos = lax.broadcasted_iota(jnp.int32, (SPAN, TOK), 1) + (2 + core) * TOK
            allowed = (
                (seg_k[core * TOK : core * TOK + SPAN] == seg[:, (2 + core) * TOK : (3 + core) * TOK])
                & (key_pos <= query_pos)
                & (key_pos >= first_key)
            )
            bias[core, row] = jnp.where(allowed, 0.0, -1e30)

    own_next.wait_recv()
    fwd_sib.start()
    own_sib.wait_recv()
    fwd_sib.wait_recv()
    for row in range(ROWS):
        tile = lat4[:, row * TOK : (row + 1) * TOK, LATENT:].reshape(WINDOW, 128)
        rope_hi[row] = pltpu.roll(tile.astype(F32), 64, 1)

    low = lax.broadcasted_iota(jnp.int32, (WINDOW, 128), 1) < 64

    def project(row, w):
        rows = pl.ds(pl.multiple_of(row * TOK, TOK), TOK)
        lat = lat4[:, rows, :].reshape(WINDOW, WIDE)
        kv = dot(lat[:, :LATENT], w[:, :256])
        ka_buf[:, :128] = kv[:, :128].astype(BF16)
        ka_buf[:, 128:] = lat[:, LATENT:]
        kb = kv[:, 128:256]
        kb_buf[:, :128] = jnp.where(low, 0.0, kb).astype(BF16)
        kb_buf[:, 128:] = jnp.where(low, kb, rope_hi[row]).astype(BF16)
        w_v = jnp.concatenate([w[:256, 256:], w[256:, 256:]], axis=1)
        vt_buf[...] = dot_nt(w_v, lat[:, :LATENT]).astype(BF16)

    def softmax(scores, mask):
        scores = scores * SCALE + mask
        weights = jnp.exp2(scores - jnp.max(scores, axis=0, keepdims=True))
        return (weights * (1.0 / jnp.sum(weights, axis=0, keepdims=True))).astype(BF16)

    def o_copy(t, row, core):
        cols = pl.ds(pl.multiple_of(source_seq(t, r, c) * PAIR_V, 128), PAIR_V)
        return remote(
            o_buf.at[t, core, row], out_ref.at[:, cols], o_s.at[t, core, row], o_r.at[t],
            at(row, z, x, core),
        )

    def step(t, carry):
        @pl.when(t > 0)
        def _():
            w_wait(t)

        @pl.when((t > 0) & (t < STEPS - 2) & (lax.rem(t, 2) == 1))
        def _():
            w_copy(t, t + 2, z_down).start()

        @pl.when((t > 0) & (t < STEPS - 2) & (lax.rem(t, 2) == 0))
        def _():
            w_copy(t, t + 2, z_up).start()

        @pl.when(t + LOOK < STEPS)
        def _():
            q_start(t + LOOK)

        pltpu.make_async_copy(q_buf.at[t], q_buf.at[t], q_r.at[t]).wait()

        for core in range(2):
            qp_buf[core] = dot(perm[core], q_buf[t, core].reshape(WINDOW, PAIR_Q)).astype(BF16)

        def one_row(row, carry):
            project(row, w_buf.at[t])
            rows = pl.ds(pl.multiple_of(row * TOK, TOK), TOK)
            q = qp_buf[:, rows, :].reshape(2 * TOK, PAIR_Q)
            for head, k_buf in ((0, ka_buf), (1, kb_buf)):
                lanes = slice(head * 128, (head + 1) * 128)
                scores = dot_nt(k_buf[...], q[:, head * 128 : head * 128 + 256])
                parts = [
                    softmax(
                        scores[core * TOK : core * TOK + SPAN, core * TOK : (core + 1) * TOK],
                        bias[core, row],
                    )
                    for core in range(2)
                ]
                empty = jnp.zeros((TOK, TOK), BF16)
                probs = jnp.concatenate(
                    [
                        jnp.concatenate([parts[0], empty], 0),
                        jnp.concatenate([empty, parts[1]], 0),
                    ],
                    1,
                )
                mixed = dot(vt_buf[lanes, :], probs)
                for core in range(2):
                    part = mixed[:, core * TOK : (core + 1) * TOK]
                    o_buf[t, core, row, :, lanes] = part.T.astype(BF16)
            for core in range(2):
                own = (row == r) & (c == core)

                @pl.when(jnp.logical_not(own))
                def _():
                    o_copy(t, row, core).start()

                @pl.when(own)
                def _():
                    cols = pl.ds(pl.multiple_of(source_seq(t, r, c) * PAIR_V, 128), PAIR_V)
                    pltpu.make_async_copy(
                        o_buf.at[t, core, row], out_ref.at[:, cols], o_r.at[t]
                    ).start()
            return carry

        lax.fori_loop(0, ROWS, one_row, 0)
        return carry

    lax.fori_loop(0, STEPS, step, 0)

    for dr in (1, 3, 2):
        lat_copy(dr).wait_send()
        seg_copy(dr).wait_send()
    tgt_copy.wait_send()
    own_next.wait_send()
    own_sib.wait_send()
    fwd_sib.wait_send()

    @pl.when(r != 0)
    def _():
        w_first.wait_send()

    def w_drain(t, carry):
        w_copy(0, t, z_down).wait_send()
        return carry

    lax.fori_loop(1, STEPS, w_drain, 0)

    def drain(t, carry):
        for i in range(7):
            q_copy(t, i).wait_send()
        for dr, dc, row, core in group:
            o_copy(t, row, core).wait_send()
        done = out_ref.at[:, pl.ds(pl.multiple_of(t * 8 * PAIR_V, 128), 8 * PAIR_V)]
        pltpu.make_async_copy(done, done, o_r.at[t]).wait()
        return carry

    lax.fori_loop(0, STEPS, drain, 0)


def local(rollout_query, rollout_latent, trainer_row, segment_ids, kv_gain, key_up, value_up):
    vmem = pl.BlockSpec(memory_space=pltpu.VMEM)
    hbm = pl.BlockSpec(memory_space=pl.ANY)
    dma = pltpu.SemaphoreType.DMA
    return pl.pallas_call(
        kernel,
        out_shape=jax.ShapeDtypeStruct((TOK, HEADS * V_HEAD), BF16),
        in_specs=[hbm] + [vmem] * 6,
        out_specs=hbm,
        scratch_shapes=[
            pltpu.VMEM((ROWS, TOK, WIDE), BF16),
            pltpu.VMEM((2, 1, WINDOW), jnp.int32),
            pltpu.VMEM((ROWS, 1, WINDOW), jnp.int32),
            pltpu.VMEM((4, WINDOW, WIDE), BF16),
            pltpu.VMEM((2, WINDOW, WINDOW), BF16),
            pltpu.VMEM((2, ROWS, SPAN, TOK), F32),
            pltpu.VMEM((ROWS, WINDOW, 128), F32),
            pltpu.VMEM((LATENT, 512), BF16),
            pltpu.VMEM((STEPS, LATENT, 512), BF16),
            pltpu.VMEM((STEPS, 2, ROWS, TOK, PAIR_Q), BF16),
            pltpu.VMEM((STEPS, 2, ROWS, TOK, PAIR_V), BF16),
            pltpu.VMEM((WINDOW, 256), BF16),
            pltpu.VMEM((WINDOW, 256), BF16),
            pltpu.VMEM((256, WINDOW), BF16),
            pltpu.VMEM((2, WINDOW, PAIR_Q), BF16),
            dma((3,)), dma((3,)), dma((3,)), dma((3,)), dma, dma, dma((3,)), dma((3,)),
            dma((STEPS,)), dma((STEPS,)), dma((STEPS, 7)), dma((STEPS,)), dma((STEPS, 2, ROWS)),
            dma((STEPS,)),
        ],
        compiler_params=pltpu.CompilerParams(
            collective_id=0, has_side_effects=True, vmem_limit_bytes=56 << 20
        ),
        cost_estimate=pl.CostEstimate(
            flops=18_000_000_000, bytes_accessed=24_000_000, transcendentals=6_500_000
        ),
    )(
        rollout_query, rollout_latent, trainer_row, segment_ids, kv_gain.reshape(1, LATENT),
        key_up, value_up,
    )


def solution(mesh):
    placed = (
        P(("rows", "seq"), None),
        P(("rows", "seq"), None),
        P(None, "seq"),
        P("rows", None),
        P(),
        P(None, "seq"),
        P(None, "seq"),
    )
    return jax.shard_map(
        local, mesh=mesh, in_specs=placed, out_specs=P(("rows", "seq"), None), check_vma=False
    )
```
